1024 devices in a mesh: row: 32 (over y, z_lo), col: 32 (over x, z_hi, core).
Axes of the slice: x: 4, y: 4, z: 32 (z_hi: 4, z_lo: 8; z = z_hi * 8 + z_lo), core: 2. Of those that a mesh axis runs over, the one named last changes fastest.
Arguments:
- amplitudes: float32 [4096, 4096], P('row', 'col'), as said below
- coupling: bfloat16 [4096, 4096], P('row', 'col')
- source: float32 [4096, 4096], P('row', 'col')
- orbital_gaps: float32 [4096], replicated, may hold values from 2 to 6
Outputs:
- new_amplitudes: float32 [4096, 4096], P('row', 'col')
- norms: float32 [3], replicated
The draws below stay inside these ranges and needn't reach their ends.
Inputs may be any that keep to these rules, and one draw needn't show every extreme that they name: amplitudes, coupling and source are symmetric matrices: entry (ia,jb) equals entry (jb,ia).
All inputs are finite; a program needn't handle non-finite values.
Results may differ from the reference program's by a relative error of at most 0.001.
Values may be sent and summed in bfloat16 or wider, within the bound.
No kernel may reach another device: no remote copies, remote signals or barrier semaphores. Data moves between devices by JAX's collectives and lax.ppermute only.
A program may use at most 32 MiB of HBM per device.

```python
import jax
import jax.numpy as jnp

NO = 16
NV = 256
ITERS = 3
M = 4096


def symmetric_normal(key, order):
    base = jax.random.normal(key, (order, order), jnp.float32)
    return (base + base.T) * 0.7071


def draw_amplitudes(key, part):
    key = jax.random.fold_in(key, 1)
    order = NO * NV
    field = symmetric_normal(key, order)
    return (0.5 * field).astype(jnp.float32)


def draw_coupling(key, part):
    key = jax.random.fold_in(key, 2)
    order = NO * NV
    field = symmetric_normal(key, order)
    return (field * order ** (-0.5)).astype(jnp.bfloat16)


def draw_source(key, part):
    key = jax.random.fold_in(key, 3)
    order = NO * NV
    first, second = jax.random.split(key)
    spread = jax.random.uniform(second, (order,), jnp.float32)
    position = jnp.arange(order, dtype=jnp.float32) / order
    field = symmetric_normal(first, order)
    scales = jnp.sqrt(1.0 + 2.0 * position) * jnp.power(10.0, 0.5 * (spread - 0.5))
    return (field * scales[:, None] * scales[None, :]).astype(jnp.float32)


def setup_inputs(seed: int = 0) -> dict:
    seeds = jax.random.split(jax.random.key(seed), 5)
    return {
        "amplitudes": draw_amplitudes(jax.random.fold_in(seeds[4], 71), 0),
        "coupling": draw_coupling(jax.random.fold_in(seeds[4], 71), 0),
        "source": draw_source(jax.random.fold_in(seeds[4], 71), 0),
        "orbital_gaps": jnp.clip(jax.random.uniform(seeds[3], (M,), jnp.float32, 2.0, 6.0), 2.0, 6.0),
    }


def reference(amplitudes, coupling, source, orbital_gaps):
    delta = orbital_gaps[:, None] + orbital_gaps[None, :]
    amps = amplitudes
    norm_list = []
    for step in range(ITERS):
        amps_low = amps.astype(jnp.bfloat16)
        cycle = jnp.dot(amps_low, coupling, preferred_element_type=jnp.float32)
        paired = cycle + cycle.T
        residual = source + delta * amps + paired + amps * paired
        norm_list.append(jnp.sqrt(jnp.sum(residual * residual)) / (NO * NV))
        amps = amps - residual / delta
    return (amps, jnp.stack(norm_list))
```

```python
import jax
import jax.numpy as jnp
from jax import lax
from jax.sharding import Mesh, PartitionSpec as P

NO = 16
NV = 256
ITERS = 3

AXES = ("y", "l", "x", "h", "c")
SIZES = (4, 8, 4, 4, 2)
SIDE = 32
ROW = ("y", "l")
COL = ("x", "h", "c")


def gather(tile, axes, count):
    copies = jnp.broadcast_to(tile[None], (count,) + tile.shape)
    return lax.all_to_all(copies, axes, 0, 0, tiled=True)


def swap(tile, axis, size, bit):
    return lax.ppermute(tile, axis, [(i, i ^ bit) for i in range(size)])


def ordered(own, other, bit):
    first = bit == 0
    return jnp.stack([jnp.where(first, own, other), jnp.where(first, other, own)])


def transpose_tiles(tile):
    pairs = [(r * SIDE + c, c * SIDE + r) for r in range(SIDE) for c in range(SIDE)]
    return lax.ppermute(tile, AXES, pairs)


def gather_amps(low):
    by_l = gather(low, "l", 8)
    by_y = gather(by_l, "y", 4)
    return by_y.reshape(-1, low.shape[1])


def body(amplitudes, coupling, source, orbital_gaps):
    n = amplitudes.shape[0]
    h = lax.axis_index("h")
    row_start = lax.axis_index(ROW) * n
    col_start = lax.axis_index(COL) * n
    gap_rows = lax.dynamic_slice_in_dim(orbital_gaps, row_start, n)
    gap_cols = lax.dynamic_slice_in_dim(orbital_gaps, col_start, n)
    delta = gap_rows[:, None] + gap_cols[None, :]

    turned = coupling.T
    far = swap(turned, "h", 4, 2)
    low = amplitudes.astype(jnp.bfloat16)
    by_l = gather(low, "l", 8)
    far, by_l = lax.optimization_barrier((far, by_l))
    pair = ordered(turned, far, h // 2)
    near = swap(pair, "h", 4, 1)
    amp_cols = gather(by_l, "y", 4).reshape(-1, n)
    near, amp_cols = lax.optimization_barrier((near, amp_cols))
    quad = jnp.swapaxes(ordered(pair, near, h % 2), 0, 1).reshape(4, n, n)
    by_x = gather(quad, "x", 4).reshape(16, n, n)
    other = swap(by_x, "c", 2, 1)
    both = ordered(by_x, other, lax.axis_index("c"))
    coupling_rows = jnp.swapaxes(both, 0, 1).reshape(-1, n)

    amps = amplitudes
    squares = []
    for step in range(ITERS):
        if step:
            amp_cols = gather_amps(amps.astype(jnp.bfloat16))
        product = lax.dot_general(
            coupling_rows,
            amp_cols,
            (((0,), (0,)), ((), ())),
            preferred_element_type=jnp.float32,
        )
        paired = product + transpose_tiles(product).T
        residual = source + delta * amps + paired + amps * paired
        squares.append(jnp.sum(residual * residual))
        amps = amps - residual / delta

    local = jnp.zeros((1, 128), jnp.float32)
    local = local.at[0, :ITERS].set(jnp.stack(squares))
    plane = jnp.sum(gather(local, ("y", "x", "c"), 32), axis=0)
    total = jnp.sum(gather(plane, ("l", "h"), 32), axis=0)
    norms = jnp.sqrt(total[0, :ITERS]) / (NO * NV)
    return (amps, norms)


def solution(mesh):
    fine = Mesh(mesh.devices.reshape(SIZES), AXES)
    in_specs = (P(ROW, COL), P(ROW, COL), P(ROW, COL), P())
    out_specs = (P(ROW, COL), P())
    return jax.shard_map(body, mesh=fine, in_specs=in_specs, out_specs=out_specs, check_vma=False)
```

```python
import jax
import jax.numpy as jnp
import numpy as np
from jax import lax
from jax.sharding import Mesh, PartitionSpec as P

NO = 16
NV = 256
ITERS = 3

AXES = ("y", "m", "p", "x", "h", "c")
SIZES = (4, 4, 2, 4, 4, 2)
ROW = ("y", "m", "p")
COL = ("x", "h", "c")
NEAR_ROW = ("y", "x", "p")
NEAR_COL = ("m", "h", "c")


def places():
    side = SIZES[0] * SIZES[1] * SIZES[2]
    grid = np.arange(side * side).reshape(SIZES)
    return grid.reshape(side, side), grid.transpose(0, 3, 2, 1, 4, 5).reshape(side, side)


def send(tile, source, target):
    pairs = list(zip(source.ravel().tolist(), target.ravel().tolist()))
    return lax.ppermute(tile, AXES, pairs)


def swap(tile, axis, bit):
    size = SIZES[AXES.index(axis)]
    return lax.ppermute(tile, axis, [(i, i ^ bit) for i in range(size)])


def gather(tiles, *axes):
    count = int(np.prod([SIZES[AXES.index(axis)] for axis in axes]))
    copies = jnp.broadcast_to(tiles[None], (count,) + tiles.shape)
    got = lax.all_to_all(copies, axes, 0, 0, tiled=True)
    return got.reshape((-1,) + tiles.shape[1:])


def ordered(own, other, bit):
    first = bit == 0
    return jnp.stack([jnp.where(first, own, other), jnp.where(first, other, own)])


def with_core(tiles):
    both = ordered(tiles, swap(tiles, "c", 1), lax.axis_index("c"))
    return jnp.swapaxes(both, 0, 1).reshape(-1, tiles.shape[-1])


def multiply(left, right):
    dims = (((0,), (0,)), ((), ()))
    return lax.dot_general(left, right, dims, preferred_element_type=jnp.float32)


def body(amplitudes, coupling, source, orbital_gaps):
    n = amplitudes.shape[0]
    start, near = places()
    h = lax.axis_index("h")

    turned = coupling.T
    far = swap(turned, "h", 2)
    low = amplitudes.astype(jnp.bfloat16)[None]
    by_m = gather(low, "m", "p")
    far, by_m = lax.optimization_barrier((far, by_m))
    pair = ordered(turned, far, h // 2)
    close = swap(pair, "h", 1)
    amp_cols = gather(by_m, "y").reshape(-1, n)
    state = send(jnp.stack([source, amplitudes]), start, near)
    close, amp_cols, state = lax.optimization_barrier((close, amp_cols, state))
    quad = jnp.swapaxes(ordered(pair, close, h % 2), 0, 1).reshape(-1, n, n)
    by_x = gather(quad, "x")
    product = multiply(with_core(by_x), amp_cols)
    later = send(by_x, start, near)
    own = send(product, start, near)
    mirror = send(product, start, near.T)
    later, own, mirror = lax.optimization_barrier((later, own, mirror))
    coupling_rows = with_core(later)
    source, amps = state[0], state[1]

    gap_rows = lax.dynamic_slice_in_dim(orbital_gaps, lax.axis_index(NEAR_ROW) * n, n)
    gap_cols = lax.dynamic_slice_in_dim(orbital_gaps, lax.axis_index(NEAR_COL) * n, n)
    delta = gap_rows[:, None] + gap_cols[None, :]
    squares = []
    for step in range(ITERS):
        if step:
            amp_cols = gather(amps.astype(jnp.bfloat16)[None], *NEAR_ROW).reshape(-1, n)
            own = multiply(coupling_rows, amp_cols)
            mirror = send(own, near, near.T)
        paired = own + mirror.T
        residual = source + delta * amps + paired + amps * paired
        squares.append(jnp.sum(residual * residual))
        amps = amps - residual / delta

    local = jnp.zeros((1, 128), jnp.float32)
    local = local.at[0, :ITERS].set(jnp.stack(squares))
    plane = jnp.sum(gather(local[None], "y", "x", "c"), axis=0)
    total = jnp.sum(gather(plane[None], "m", "p", "h"), axis=0)
    norms = jnp.sqrt(total[0, :ITERS]) / (NO * NV)
    return (send(amps, near, start), norms)


def solution(mesh):
    fine = Mesh(mesh.devices.reshape(SIZES), AXES)
    in_specs = (P(ROW, COL), P(ROW, COL), P(ROW, COL), P())
    out_specs = (P(ROW, COL), P())
    return jax.shard_map(body, mesh=fine, in_specs=in_specs, out_specs=out_specs, check_vma=False)
```

```python
import jax
import jax.numpy as jnp
from jax import lax
from jax.sharding import Mesh, PartitionSpec as P

NO = 16
NV = 256
ITERS = 3

AXES = ("y", "l", "x", "h", "c")
SIZES = (4, 8, 4, 4, 2)
SIDE = 32
ROW = ("y", "l")
COL = ("x", "h", "c")


def gather(tile, axes, count):
    copies = jnp.broadcast_to(tile[None], (count,) + tile.shape)
    return lax.all_to_all(copies, axes, 0, 0, tiled=True)


def swap(tile, axis, size, bit):
    return lax.ppermute(tile, axis, [(i, i ^ bit) for i in range(size)])


def ordered(own, other, bit):
    first = bit == 0
    return jnp.stack([jnp.where(first, own, other), jnp.where(first, other, own)])


def transpose_tiles(tile):
    pairs = [(r * SIDE + c, c * SIDE + r) for r in range(SIDE) for c in range(SIDE)]
    return lax.ppermute(tile, AXES, pairs)


def body(amplitudes, coupling, source, orbital_gaps):
    n = amplitudes.shape[0]
    h = lax.axis_index("h")
    row_start = lax.axis_index(ROW) * n
    col_start = lax.axis_index(COL) * n
    gap_rows = lax.dynamic_slice_in_dim(orbital_gaps, row_start, n)
    gap_cols = lax.dynamic_slice_in_dim(orbital_gaps, col_start, n)
    delta = gap_rows[:, None] + gap_cols[None, :]

    turned = coupling.T
    far = swap(turned, "h", 4, 2)
    low = amplitudes.astype(jnp.bfloat16)
    by_l = gather(low, "l", 8)
    far, by_l = lax.optimization_barrier((far, by_l))
    pair = ordered(turned, far, h // 2)
    near = swap(pair, "h", 4, 1)
    amp_cols = gather(by_l, "y", 4).reshape(-1, n)
    near, amp_cols = lax.optimization_barrier((near, amp_cols))
    quad = jnp.swapaxes(ordered(pair, near, h % 2), 0, 1).reshape(4, n, n)
    by_x = gather(quad, "x", 4).reshape(16, n, n)
    other = swap(by_x, "c", 2, 1)
    both = ordered(by_x, other, lax.axis_index("c"))
    coupling_rows = jnp.swapaxes(both, 0, 1).reshape(-1, n)

    amps = amplitudes
    squares = []
    for step in range(ITERS):
        if step:
            by_l = gather(amps.astype(jnp.bfloat16), "l", 8).reshape(-1, n)
            shares = jnp.einsum("ykr,kc->yrc", coupling_part, by_l, preferred_element_type=jnp.float32)
            product = jnp.sum(lax.all_to_all(shares, "y", 0, 0, tiled=True), axis=0)
            mirror = transpose_tiles(product)
        else:
            product = lax.dot_general(
                coupling_rows,
                amp_cols,
                (((0,), (0,)), ((), ())),
                preferred_element_type=jnp.float32,
            )
            mirror = transpose_tiles(product)
            parts = coupling_rows.reshape(4, -1, n)
            coupling_part = lax.all_to_all(parts, "y", 0, 0, tiled=True)
            mirror, coupling_part = lax.optimization_barrier((mirror, coupling_part))
        paired = product + mirror.T
        residual = source + delta * amps + paired + amps * paired
        squares.append(jnp.sum(residual * residual))
        amps = amps - residual / delta

    local = jnp.zeros((1, 128), jnp.float32)
    local = local.at[0, :ITERS].set(jnp.stack(squares))
    plane = jnp.sum(gather(local, ("y", "x", "c"), 32), axis=0)
    total = jnp.sum(gather(plane, ("l", "h"), 32), axis=0)
    norms = jnp.sqrt(total[0, :ITERS]) / (NO * NV)
    return (amps, norms)


def solution(mesh):
    fine = Mesh(mesh.devices.reshape(SIZES), AXES)
    in_specs = (P(ROW, COL), P(ROW, COL), P(ROW, COL), P())
    out_specs = (P(ROW, COL), P())
    return jax.shard_map(body, mesh=fine, in_specs=in_specs, out_specs=out_specs, check_vma=False)
```

```python
import jax
import jax.numpy as jnp
from jax import lax
from jax.sharding import Mesh, PartitionSpec as P

NO = 16
NV = 256
ITERS = 3

AXES = ("y", "l", "x", "h", "c")
SIZES = (4, 8, 4, 4, 2)
SIDE = 32
ROW = ("y", "l")
COL = ("x", "h", "c")


def gather(tile, axes, count):
    copies = jnp.broadcast_to(tile[None], (count,) + tile.shape)
    return lax.all_to_all(copies, axes, 0, 0, tiled=True)


def swap(tile, axis, size, bit):
    return lax.ppermute(tile, axis, [(i, i ^ bit) for i in range(size)])


def ordered(own, other, bit):
    first = bit == 0
    return jnp.stack([jnp.where(first, own, other), jnp.where(first, other, own)])


def transpose_tiles(tile):
    pairs = [(r * SIDE + c, c * SIDE + r) for r in range(SIDE) for c in range(SIDE)]
    return lax.ppermute(tile, AXES, pairs)


def body(amplitudes, coupling, source, orbital_gaps):
    n = amplitudes.shape[0]
    h = lax.axis_index("h")
    row_start = lax.axis_index(ROW) * n
    col_start = lax.axis_index(COL) * n
    gap_rows = lax.dynamic_slice_in_dim(orbital_gaps, row_start, n)
    gap_cols = lax.dynamic_slice_in_dim(orbital_gaps, col_start, n)
    delta = gap_rows[:, None] + gap_cols[None, :]

    turned = coupling.T
    far = swap(turned, "h", 4, 2)
    low = amplitudes.astype(jnp.bfloat16)
    by_l = gather(low, "l", 8)
    far, by_l = lax.optimization_barrier((far, by_l))
    pair = ordered(turned, far, h // 2)
    near = swap(pair, "h", 4, 1)
    amp_cols = gather(by_l, "y", 4).reshape(-1, n)
    near, amp_cols = lax.optimization_barrier((near, amp_cols))
    quad = jnp.swapaxes(ordered(pair, near, h % 2), 0, 1).reshape(4, n, n)
    by_x = gather(quad, "x", 4).reshape(16, n, n)
    other = swap(by_x, "c", 2, 1)
    both = ordered(by_x, other, lax.axis_index("c"))
    coupling_rows = jnp.swapaxes(both, 0, 1).reshape(-1, n)

    amps = amplitudes
    squares = []
    for step in range(ITERS):
        if step:
            by_l = gather(amps.astype(jnp.bfloat16), "l", 8).reshape(-1, n)
            shares = jnp.einsum("ykr,kc->yrc", coupling_part, by_l, preferred_element_type=jnp.float32)
            product = jnp.sum(lax.all_to_all(shares, "y", 0, 0, tiled=True), axis=0)
            mirror = transpose_tiles(product)
        else:
            product = lax.dot_general(
                coupling_rows,
                amp_cols,
                (((0,), (0,)), ((), ())),
                preferred_element_type=jnp.float32,
            )
            product, coupling_rows = lax.optimization_barrier((product, coupling_rows))
            mirror = transpose_tiles(product)
            parts = coupling_rows.reshape(4, -1, n)
            coupling_part = lax.all_to_all(parts, "y", 0, 0, tiled=True)
            mirror, coupling_part = lax.optimization_barrier((mirror, coupling_part))
        paired = product + mirror.T
        residual = source + delta * amps + paired + amps * paired
        squares.append(jnp.sum(residual * residual))
        amps = amps - residual / delta

    amps, squares = lax.optimization_barrier((amps, squares))
    lane = lax.broadcasted_iota(jnp.int32, (1, 128), 1)
    local = jnp.zeros((1, 128), jnp.float32)
    for step, square in enumerate(squares):
        local = jnp.where(lane == step, square, local)
    plane = jnp.sum(gather(local, ("y", "x", "c"), 32), axis=0)
    total = jnp.sum(gather(plane, ("l", "h"), 32), axis=0)
    norms = jnp.sqrt(total[0, :ITERS]) / (NO * NV)
    return (amps, norms)


def solution(mesh):
    fine = Mesh(mesh.devices.reshape(SIZES), AXES)
    in_specs = (P(ROW, COL), P(ROW, COL), P(ROW, COL), P())
    out_specs = (P(ROW, COL), P())
    return jax.shard_map(body, mesh=fine, in_specs=in_specs, out_specs=out_specs, check_vma=False)
```

```python
import jax
import jax.numpy as jnp
import numpy as np
from jax import lax
from jax.sharding import Mesh, PartitionSpec as P

NO = 16
NV = 256
ITERS = 3

AXES = ("y", "l", "x", "h", "c")
SIZES = (4, 8, 4, 4, 2)
SIDE = 32
ROW = ("y", "l")
COL = ("x", "h", "c")


def gather(tile, axes, count):
    copies = jnp.broadcast_to(tile[None], (count,) + tile.shape)
    return lax.all_to_all(copies, axes, 0, 0, tiled=True)


def swap(tile, axis, size, bit):
    return lax.ppermute(tile, axis, [(i, i ^ bit) for i in range(size)])


def ordered(own, other, bit):
    first = bit == 0
    return jnp.stack([jnp.where(first, own, other), jnp.where(first, other, own)])


def places():
    grid = np.arange(SIDE * SIDE).reshape(SIZES)
    return grid.reshape(SIDE, SIDE), grid.transpose(2, 1, 0, 3, 4).reshape(SIDE, SIDE)


def send(tile, source, target):
    return lax.ppermute(tile, AXES, list(zip(source.ravel().tolist(), target.ravel().tolist())))


def body(amplitudes, coupling, source, orbital_gaps):
    n = amplitudes.shape[0]
    h = lax.axis_index("h")
    start, turned = places()

    block = coupling.T
    far = swap(block, "h", 4, 2)
    low = send(amplitudes.astype(jnp.bfloat16), start, turned)
    far, low = lax.optimization_barrier((far, low))
    pair = ordered(block, far, h // 2)
    near = swap(pair, "h", 4, 1)
    by_l = gather(low, "l", 8).reshape(-1, n)
    near, by_l = lax.optimization_barrier((near, by_l))
    state = send(jnp.stack([source, amplitudes]), start, turned)
    quad = jnp.swapaxes(ordered(pair, near, h % 2), 0, 1).reshape(4, n, n)
    by_y = gather(quad, "y", 4).reshape(16, n, n)
    other = swap(by_y, "c", 2, 1)
    both = ordered(by_y, other, lax.axis_index("c"))
    part = jnp.swapaxes(both, 0, 1).reshape(4, -1, n)

    source, amps = state[0], state[1]
    gap_rows = lax.dynamic_slice_in_dim(orbital_gaps, lax.axis_index(("x", "l")) * n, n)
    gap_cols = lax.dynamic_slice_in_dim(orbital_gaps, lax.axis_index(("y", "h", "c")) * n, n)
    delta = gap_rows[:, None] + gap_cols[None, :]
    squares = []
    for step in range(ITERS):
        if step:
            by_l = gather(amps.astype(jnp.bfloat16), "l", 8).reshape(-1, n)
        shares = jnp.einsum("ykr,kc->yrc", part, by_l, preferred_element_type=jnp.float32)
        product = jnp.sum(lax.all_to_all(shares, "x", 0, 0, tiled=True), axis=0)
        paired = product + send(product, turned, turned.T).T
        residual = source + delta * amps + paired + amps * paired
        squares.append(jnp.sum(residual * residual))
        amps = amps - residual / delta

    lane = lax.broadcasted_iota(jnp.int32, (1, 128), 1)
    local = jnp.zeros((1, 128), jnp.float32)
    for step, square in enumerate(squares):
        local = jnp.where(lane == step, square, local)
    plane = jnp.sum(gather(local, ("y", "x", "c"), 32), axis=0)
    total = jnp.sum(gather(plane, ("l", "h"), 32), axis=0)
    norms = jnp.sqrt(total[0, :ITERS]) / (NO * NV)
    return (send(amps, turned, start), norms)


def solution(mesh):
    fine = Mesh(mesh.devices.reshape(SIZES), AXES)
    in_specs = (P(ROW, COL), P(ROW, COL), P(ROW, COL), P())
    out_specs = (P(ROW, COL), P())
    return jax.shard_map(body, mesh=fine, in_specs=in_specs, out_specs=out_specs, check_vma=False)
```

```python
import jax
import jax.numpy as jnp
import numpy as np
from jax import lax
from jax.sharding import Mesh, PartitionSpec as P

NO = 16
NV = 256
ITERS = 3

AXES = ("y", "l", "x", "h", "c")
SIZES = (4, 8, 4, 4, 2)
SIDE = 32
ROW = ("y", "l")
COL = ("x", "h", "c")
SHIFT = (0, 0, 0, 2)


def gather(tile, axes, count):
    copies = jnp.broadcast_to(tile[None], (count,) + tile.shape)
    return lax.all_to_all(copies, axes, 0, 0, tiled=True)


def swap(tile, axis, size, bit):
    return lax.ppermute(tile, axis, [(i, i ^ bit) for i in range(size)])


def ordered(own, other, bit):
    first = bit == 0
    return jnp.stack([jnp.where(first, own, other), jnp.where(first, other, own)])


def places():
    grid = np.arange(SIDE * SIDE).reshape(SIZES)
    later = np.zeros(SIZES, np.int64)
    for y, l, x, h, c in np.ndindex(SIZES):
        later[y, l, x, h, c] = grid[(x + SHIFT[h]) % SIZES[0], l, y, h, c]
    return grid.reshape(SIDE, SIDE), later.reshape(SIDE, SIDE)


def send(tile, source, target):
    return lax.ppermute(tile, AXES, list(zip(source.ravel().tolist(), target.ravel().tolist())))


def body(amplitudes, coupling, source, orbital_gaps):
    n = amplitudes.shape[0]
    h = lax.axis_index("h")
    start, turned = places()

    block = coupling.T
    low = send(amplitudes.astype(jnp.bfloat16), start, turned)
    quad = gather(block, "h", 4)
    low, quad = lax.optimization_barrier((low, quad))
    by_y = gather(quad.reshape(4, n, n), "y", 4).reshape(16, n, n)
    by_y, low = lax.optimization_barrier((by_y, low))
    by_l = gather(low, "l", 8).reshape(-1, n)
    state = send(jnp.stack([source, amplitudes]), start, turned)
    other = swap(by_y, "c", 2, 1)
    both = ordered(by_y, other, lax.axis_index("c"))
    part = jnp.swapaxes(both, 0, 1).reshape(4, -1, n)

    source, amps = state[0], state[1]
    gap_rows = lax.dynamic_slice_in_dim(orbital_gaps, lax.axis_index(("x", "l")) * n, n)
    shift = sum(jnp.where(h == i, SHIFT[i], 0) for i in range(SIZES[3]))
    col = (lax.axis_index("y") - shift + 4) % 4 * 8 + lax.axis_index(("h", "c"))
    gap_cols = lax.dynamic_slice_in_dim(orbital_gaps, col * n, n)
    delta = gap_rows[:, None] + gap_cols[None, :]
    squares = []
    for step in range(ITERS):
        if step:
            by_l = gather(amps.astype(jnp.bfloat16), "l", 8).reshape(-1, n)
        shares = jnp.einsum("ykr,kc->yrc", part, by_l, preferred_element_type=jnp.float32)
        product = jnp.sum(lax.all_to_all(shares, "x", 0, 0, tiled=True), axis=0)
        paired = product + send(product, turned, turned.T).T
        residual = source + delta * amps + paired + amps * paired
        squares.append(jnp.sum(residual * residual))
        amps = amps - residual / delta

    lane = lax.broadcasted_iota(jnp.int32, (1, 128), 1)
    local = jnp.zeros((1, 128), jnp.float32)
    for step, square in enumerate(squares):
        local = jnp.where(lane == step, square, local)
    plane = jnp.sum(gather(local, ("y", "x", "c"), 32), axis=0)
    total = jnp.sum(gather(plane, ("l", "h"), 32), axis=0)
    norms = jnp.sqrt(total[0, :ITERS]) / (NO * NV)
    return (send(amps, turned, start), norms)


def solution(mesh):
    fine = Mesh(mesh.devices.reshape(SIZES), AXES)
    in_specs = (P(ROW, COL), P(ROW, COL), P(ROW, COL), P())
    out_specs = (P(ROW, COL), P())
    return jax.shard_map(body, mesh=fine, in_specs=in_specs, out_specs=out_specs, check_vma=False)
```

```python
import jax
import jax.numpy as jnp
import numpy as np
from jax import lax
from jax.sharding import Mesh, PartitionSpec as P

NO = 16
NV = 256
ITERS = 3

AXES = ("y", "l", "x", "h", "c")
SIZES = (4, 8, 4, 4, 2)
SIDE = 32
ROW = ("y", "l")
COL = ("x", "h", "c")
SHIFT = (0, 0, 0, 2)


def gather(tile, axes, count):
    copies = jnp.broadcast_to(tile[None], (count,) + tile.shape)
    return lax.all_to_all(copies, axes, 0, 0, tiled=True)


def swap(tile, axis, size, bit):
    return lax.ppermute(tile, axis, [(i, i ^ bit) for i in range(size)])


def ordered(own, other, bit):
    first = bit == 0
    return jnp.stack([jnp.where(first, own, other), jnp.where(first, other, own)])


def places():
    grid = np.arange(SIDE * SIDE).reshape(SIZES)
    later = np.zeros(SIZES, np.int64)
    for y, l, x, h, c in np.ndindex(SIZES):
        later[y, l, x, h, c] = grid[(x + SHIFT[h]) % SIZES[0], l, y, h, c]
    return grid.reshape(SIDE, SIDE), later.reshape(SIDE, SIDE)


def send(tile, source, target):
    return lax.ppermute(tile, AXES, list(zip(source.ravel().tolist(), target.ravel().tolist())))


def body(amplitudes, coupling, source, orbital_gaps):
    n = amplitudes.shape[0]
    h = lax.axis_index("h")
    start, turned = places()

    block = coupling.T
    l = lax.axis_index("l")
    low = amplitudes.astype(jnp.bfloat16)
    across = turned[np.arange(SIDE) ^ 4]
    own, other = send(low, start, turned), send(low, start, across)
    quad = lax.all_gather(block, "h")
    own, other, quad = lax.optimization_barrier((own, other, quad))
    two = ordered(own, other, l // 4)
    other = swap(two, "l", 8, 2)
    by_y = lax.all_gather(quad, "y").reshape(16, n, n)
    other, by_y = lax.optimization_barrier((other, by_y))
    four = jnp.swapaxes(ordered(two, other, l // 2 % 2), 0, 1).reshape(4, n, n)
    eight = ordered(four, swap(four, "l", 8, 1), l % 2)
    by_l = jnp.swapaxes(eight, 0, 1).reshape(-1, n)
    state = send(jnp.stack([source, amplitudes]), start, turned)
    other = swap(by_y, "c", 2, 1)
    both = ordered(by_y, other, lax.axis_index("c"))
    part = jnp.swapaxes(both, 0, 1).reshape(4, -1, n)

    source, amps = state[0], state[1]
    gap_rows = lax.dynamic_slice_in_dim(orbital_gaps, lax.axis_index(("x", "l")) * n, n)
    shift = sum(jnp.where(h == i, SHIFT[i], 0) for i in range(SIZES[3]))
    col = (lax.axis_index("y") - shift + 4) % 4 * 8 + lax.axis_index(("h", "c"))
    gap_cols = lax.dynamic_slice_in_dim(orbital_gaps, col * n, n)
    delta = gap_rows[:, None] + gap_cols[None, :]
    squares = []
    for step in range(ITERS):
        if step:
            by_l = gather(amps.astype(jnp.bfloat16), "l", 8).reshape(-1, n)
        shares = jnp.einsum("ykr,kc->yrc", part, by_l, preferred_element_type=jnp.float32)
        product = jnp.sum(lax.all_to_all(shares, "x", 0, 0, tiled=True), axis=0)
        paired = product + send(product, turned, turned.T).T
        residual = source + delta * amps + paired + amps * paired
        squares.append(jnp.sum(residual * residual))
        amps = amps - residual / delta

    lane = lax.broadcasted_iota(jnp.int32, (1, 128), 1)
    local = jnp.zeros((1, 128), jnp.float32)
    for step, square in enumerate(squares):
        local = jnp.where(lane == step, square, local)
    plane = jnp.sum(gather(local, ("y", "x", "c"), 32), axis=0)
    total = jnp.sum(gather(plane, ("l", "h"), 32), axis=0)
    norms = jnp.sqrt(total[0, :ITERS]) / (NO * NV)
    return (send(amps, turned, start), norms)


def solution(mesh):
    fine = Mesh(mesh.devices.reshape(SIZES), AXES)
    in_specs = (P(ROW, COL), P(ROW, COL), P(ROW, COL), P())
    out_specs = (P(ROW, COL), P())
    return jax.shard_map(body, mesh=fine, in_specs=in_specs, out_specs=out_specs, check_vma=False)
```

```python
import jax
import jax.numpy as jnp
import numpy as np
from jax import lax
from jax.sharding import Mesh, PartitionSpec as P

NO = 16
NV = 256
ITERS = 3

AXES = ("y", "l", "x", "h", "c")
SIZES = (4, 8, 4, 4, 2)
SIDE = 32
ROW = ("y", "l")
COL = ("x", "h", "c")
SHIFT = (0, 0, 0, 2)


def gather(tile, axes, count):
    copies = jnp.broadcast_to(tile[None], (count,) + tile.shape)
    return lax.all_to_all(copies, axes, 0, 0, tiled=True)


def swap(tile, axis, size, bit):
    return lax.ppermute(tile, axis, [(i, i ^ bit) for i in range(size)])


def ordered(own, other, bit):
    first = bit == 0
    return jnp.stack([jnp.where(first, own, other), jnp.where(first, other, own)])


def places():
    grid = np.arange(SIDE * SIDE).reshape(SIZES)
    later = np.zeros(SIZES, np.int64)
    for y, l, x, h, c in np.ndindex(SIZES):
        later[y, l, x, h, c] = grid[(x + SHIFT[h]) % SIZES[0], l, y, h, c]
    return grid.reshape(SIDE, SIDE), later.reshape(SIDE, SIDE)


def send(tile, source, target):
    return lax.ppermute(tile, AXES, list(zip(source.ravel().tolist(), target.ravel().tolist())))


def body(amplitudes, coupling, source, orbital_gaps):
    n = amplitudes.shape[0]
    h = lax.axis_index("h")
    start, turned = places()

    block = coupling.T
    l = lax.axis_index("l")
    low = amplitudes.astype(jnp.bfloat16)
    across = turned[np.arange(SIDE) ^ 4]
    own, other = send(low, start, turned), send(low, start, across)
    two = ordered(own, other, l // 4)
    other = swap(two, "l", 8, 2)
    quad = gather(block, "h", 4).reshape(4, n, n)
    two, other, quad = lax.optimization_barrier((two, other, quad))
    four = jnp.swapaxes(ordered(two, other, l // 2 % 2), 0, 1).reshape(4, n, n)
    other = swap(four, "l", 8, 1)
    by_y = gather(quad, "y", 4).reshape(16, n, n)
    state = send(jnp.stack([source, amplitudes]), start, turned)
    four, other, by_y, state = lax.optimization_barrier((four, other, by_y, state))
    eight = ordered(four, other, l % 2)
    by_l = jnp.swapaxes(eight, 0, 1).reshape(-1, n)
    other = swap(by_y, "c", 2, 1)
    both = ordered(by_y, other, lax.axis_index("c"))
    part = jnp.swapaxes(both, 0, 1).reshape(4, -1, n)

    source, amps = state[0], state[1]
    gap_rows = lax.dynamic_slice_in_dim(orbital_gaps, lax.axis_index(("x", "l")) * n, n)
    shift = sum(jnp.where(h == i, SHIFT[i], 0) for i in range(SIZES[3]))
    col = (lax.axis_index("y") - shift + 4) % 4 * 8 + lax.axis_index(("h", "c"))
    gap_cols = lax.dynamic_slice_in_dim(orbital_gaps, col * n, n)
    delta = gap_rows[:, None] + gap_cols[None, :]
    squares = []
    for step in range(ITERS):
        if step:
            by_l = gather(amps.astype(jnp.bfloat16), "l", 8).reshape(-1, n)
        shares = jnp.einsum("ykr,kc->yrc", part, by_l, preferred_element_type=jnp.float32)
        product = jnp.sum(lax.all_to_all(shares, "x", 0, 0, tiled=True), axis=0)
        paired = product + send(product, turned, turned.T).T
        residual = source + delta * amps + paired + amps * paired
        squares.append(jnp.sum(residual * residual))
        amps = amps - residual / delta

    lane = lax.broadcasted_iota(jnp.int32, (1, 128), 1)
    local = jnp.zeros((1, 128), jnp.float32)
    for step, square in enumerate(squares):
        local = jnp.where(lane == step, square, local)
    plane = jnp.sum(gather(local, ("y", "x", "c"), 32), axis=0)
    total = jnp.sum(gather(plane, ("l", "h"), 32), axis=0)
    norms = jnp.sqrt(total[0, :ITERS]) / (NO * NV)
    return (send(amps, turned, start), norms)


def solution(mesh):
    fine = Mesh(mesh.devices.reshape(SIZES), AXES)
    in_specs = (P(ROW, COL), P(ROW, COL), P(ROW, COL), P())
    out_specs = (P(ROW, COL), P())
    return jax.shard_map(body, mesh=fine, in_specs=in_specs, out_specs=out_specs, check_vma=False)
```

```python
import jax
import jax.numpy as jnp
import numpy as np
from jax import lax
from jax.sharding import Mesh, PartitionSpec as P

NO = 16
NV = 256
ITERS = 3

AXES = ("y", "l", "x", "h", "c")
SIZES = (4, 8, 4, 4, 2)
SIDE = 32
ROW = ("y", "l")
COL = ("x", "h", "c")
SHIFT = (0, 0, 0, 2)


def gather(tile, axes, count):
    copies = jnp.broadcast_to(tile[None], (count,) + tile.shape)
    return lax.all_to_all(copies, axes, 0, 0, tiled=True)


def swap(tile, axis, size, bit):
    return lax.ppermute(tile, axis, [(i, i ^ bit) for i in range(size)])


def ordered(own, other, bit):
    first = bit == 0
    return jnp.stack([jnp.where(first, own, other), jnp.where(first, other, own)])


def places():
    grid = np.arange(SIDE * SIDE).reshape(SIZES)
    later = np.zeros(SIZES, np.int64)
    for y, l, x, h, c in np.ndindex(SIZES):
        later[y, l, x, h, c] = grid[(x + SHIFT[h]) % SIZES[0], l, y, h, c]
    return grid.reshape(SIDE, SIDE), later.reshape(SIDE, SIDE)


def send(tile, source, target):
    return lax.ppermute(tile, AXES, list(zip(source.ravel().tolist(), target.ravel().tolist())))


def body(amplitudes, coupling, source, orbital_gaps):
    n = amplitudes.shape[0]
    h = lax.axis_index("h")
    start, turned = places()

    block = coupling.T
    l = lax.axis_index("l")
    low = amplitudes.astype(jnp.bfloat16)
    across = turned[np.arange(SIDE) ^ 4]
    own, other = send(low, start, turned), send(low, start, across)
    two = ordered(own, other, l // 4)
    other = swap(two, "l", 8, 2)
    quad = gather(block, "h", 4).reshape(4, n, n)
    two, other, quad = lax.optimization_barrier((two, other, quad))
    four = jnp.swapaxes(ordered(two, other, l // 2 % 2), 0, 1).reshape(4, n, n)
    other = swap(four, "l", 8, 1)
    by_y = gather(quad, "y", 4).reshape(16, n, n)
    state = send(jnp.stack([source, amplitudes]), start, turned)
    four, other, by_y, state = lax.optimization_barrier((four, other, by_y, state))
    eight = ordered(four, other, l % 2)
    by_l = jnp.swapaxes(eight, 0, 1).reshape(-1, n)
    other = swap(by_y, "c", 2, 1)
    both = ordered(by_y, other, lax.axis_index("c"))
    part = jnp.swapaxes(both, 0, 1).reshape(4, -1, n)

    source, amps = state[0], state[1]
    gap_rows = lax.dynamic_slice_in_dim(orbital_gaps, lax.axis_index(("x", "l")) * n, n)
    shift = sum(jnp.where(h == i, SHIFT[i], 0) for i in range(SIZES[3]))
    col = (lax.axis_index("y") - shift + 4) % 4 * 8 + lax.axis_index(("h", "c"))
    gap_cols = lax.dynamic_slice_in_dim(orbital_gaps, col * n, n)
    delta = gap_rows[:, None] + gap_cols[None, :]
    lane = lax.broadcasted_iota(jnp.int32, (1, 128), 1)
    local = jnp.zeros((1, 128), jnp.float32)
    for step in range(ITERS):
        if step:
            by_l = gather(amps.astype(jnp.bfloat16), "l", 8).reshape(-1, n)
        shares = jnp.einsum("ykr,kc->yrc", part, by_l, preferred_element_type=jnp.float32)
        product = jnp.sum(lax.all_to_all(shares, "x", 0, 0, tiled=True), axis=0)
        paired = product + send(product, turned, turned.T).T
        residual = source + delta * amps + paired + amps * paired
        square = jnp.sum(jnp.sum(residual * residual, axis=0, keepdims=True), axis=1, keepdims=True)
        local = jnp.where(lane == step, square, local)
        amps = amps - residual / delta
        if step < ITERS - 1:
            amps, local = lax.optimization_barrier((amps, local))

    plane = jnp.sum(gather(local, ("y", "x", "c"), 32), axis=0)
    total = jnp.sum(gather(plane, ("l", "h"), 32), axis=0)
    norms = jnp.sqrt(total[0, :ITERS]) / (NO * NV)
    return (send(amps, turned, start), norms)


def solution(mesh):
    fine = Mesh(mesh.devices.reshape(SIZES), AXES)
    in_specs = (P(ROW, COL), P(ROW, COL), P(ROW, COL), P())
    out_specs = (P(ROW, COL), P())
    return jax.shard_map(body, mesh=fine, in_specs=in_specs, out_specs=out_specs, check_vma=False)
```

```python
import jax
import jax.numpy as jnp
import numpy as np
from jax import lax
from jax.sharding import Mesh, PartitionSpec as P

NO = 16
NV = 256
ITERS = 3

AXES = ("y", "l", "x", "h", "c")
SIZES = (4, 8, 4, 4, 2)
SIDE = 32
ROW = ("y", "l")
COL = ("x", "h", "c")
SHIFT = (0, 0, 0, 2)


def gather(tile, axes, count):
    copies = jnp.broadcast_to(tile[None], (count,) + tile.shape)
    return lax.all_to_all(copies, axes, 0, 0, tiled=True)


def swap(tile, axis, size, bit):
    return lax.ppermute(tile, axis, [(i, i ^ bit) for i in range(size)])


def ordered(own, other, bit):
    first = bit == 0
    return jnp.stack([jnp.where(first, own, other), jnp.where(first, other, own)])


def places():
    grid = np.arange(SIDE * SIDE).reshape(SIZES)
    later = np.zeros(SIZES, np.int64)
    for y, l, x, h, c in np.ndindex(SIZES):
        later[y, l, x, h, c] = grid[(x + SHIFT[h]) % SIZES[0], l, y, h, c]
    return grid.reshape(SIDE, SIDE), later.reshape(SIDE, SIDE)


def send(tile, source, target):
    return lax.ppermute(tile, AXES, list(zip(source.ravel().tolist(), target.ravel().tolist())))


def body(amplitudes, coupling, source, orbital_gaps):
    n = amplitudes.shape[0]
    h = lax.axis_index("h")
    start, turned = places()

    block = coupling.T
    l = lax.axis_index("l")
    low = amplitudes.astype(jnp.bfloat16)
    across = turned[np.arange(SIDE) ^ 4]
    own, other = send(low, start, turned), send(low, start, across)
    two = ordered(own, other, l // 4)
    other = swap(two, "l", 8, 2)
    quad = gather(block, "h", 4).reshape(4, n, n)
    two, other, quad = lax.optimization_barrier((two, other, quad))
    four = jnp.swapaxes(ordered(two, other, l // 2 % 2), 0, 1).reshape(4, n, n)
    other = swap(four, "l", 8, 1)
    by_y = gather(quad, "y", 4).reshape(16, n, n)
    four, other, by_y = lax.optimization_barrier((four, other, by_y))
    eight = ordered(four, other, l % 2)
    by_l = jnp.swapaxes(eight, 0, 1).reshape(-1, n)
    other = swap(by_y, "c", 2, 1)
    both = ordered(by_y, other, lax.axis_index("c"))
    part = jnp.swapaxes(both, 0, 1).reshape(4, -1, n)

    state = send(jnp.stack([source, amplitudes]), start, turned)
    source, amps = state[0], state[1]
    gap_rows = lax.dynamic_slice_in_dim(orbital_gaps, lax.axis_index(("x", "l")) * n, n)
    shift = sum(jnp.where(h == i, SHIFT[i], 0) for i in range(SIZES[3]))
    col = (lax.axis_index("y") - shift + 4) % 4 * 8 + lax.axis_index(("h", "c"))
    gap_cols = lax.dynamic_slice_in_dim(orbital_gaps, col * n, n)
    delta = gap_rows[:, None] + gap_cols[None, :]
    lane = lax.broadcasted_iota(jnp.int32, (1, 128), 1)
    local = jnp.zeros((1, 128), jnp.float32)
    for step in range(ITERS):
        if step:
            by_l = gather(amps.astype(jnp.bfloat16), "l", 8).reshape(-1, n)
        shares = jnp.einsum("ykr,kc->yrc", part, by_l, preferred_element_type=jnp.float32)
        product = jnp.sum(lax.all_to_all(shares, "x", 0, 0, tiled=True), axis=0)
        mirror = send(product, turned, turned.T)
        if step:
            local = jnp.where(lane == step - 1, square, local)
            mirror, local = lax.optimization_barrier((mirror, local))
        paired = product + mirror.T
        residual = source + delta * amps + paired + amps * paired
        square = jnp.sum(residual * residual)
        amps = amps - residual / delta

    local = jnp.where(lane == ITERS - 1, square, local)
    plane = jnp.sum(gather(local, ("y", "x", "c"), 32), axis=0)
    total = jnp.sum(gather(plane, ("l", "h"), 32), axis=0)
    norms = jnp.sqrt(total[0, :ITERS]) / (NO * NV)
    return (send(amps, turned, start), norms)


def solution(mesh):
    fine = Mesh(mesh.devices.reshape(SIZES), AXES)
    in_specs = (P(ROW, COL), P(ROW, COL), P(ROW, COL), P())
    out_specs = (P(ROW, COL), P())
    return jax.shard_map(body, mesh=fine, in_specs=in_specs, out_specs=out_specs, check_vma=False)
```

```python
import jax
import jax.numpy as jnp
import numpy as np
from jax import lax
from jax.sharding import Mesh, PartitionSpec as P

NO = 16
NV = 256
ITERS = 3

AXES = ("y", "l", "x", "h", "c")
SIZES = (4, 8, 4, 4, 2)
SIDE = 32
ROW = ("y", "l")
COL = ("x", "h", "c")
SHIFT = (0, 0, 0, 2)


def gather(tile, axes, count):
    copies = jnp.broadcast_to(tile[None], (count,) + tile.shape)
    return lax.all_to_all(copies, axes, 0, 0, tiled=True)


def swap(tile, axis, size, bit):
    return lax.ppermute(tile, axis, [(i, i ^ bit) for i in range(size)])


def ordered(own, other, bit):
    first = bit == 0
    return jnp.stack([jnp.where(first, own, other), jnp.where(first, other, own)])


def places():
    grid = np.arange(SIDE * SIDE).reshape(SIZES)
    later = np.zeros(SIZES, np.int64)
    for y, l, x, h, c in np.ndindex(SIZES):
        later[y, l, x, h, c] = grid[(x + SHIFT[h]) % SIZES[0], l, y, h, c]
    return grid.reshape(SIDE, SIDE), later.reshape(SIDE, SIDE)


def send(tile, source, target):
    return lax.ppermute(tile, AXES, list(zip(source.ravel().tolist(), target.ravel().tolist())))


def body(amplitudes, coupling, source, orbital_gaps):
    n = amplitudes.shape[0]
    h = lax.axis_index("h")
    start, turned = places()

    block = coupling.T
    l = lax.axis_index("l")
    low = amplitudes.astype(jnp.bfloat16)
    across = turned[np.arange(SIDE) ^ 4]
    other = send(low, start, across)
    state = send(jnp.stack([source, amplitudes]), start, turned)
    source, amps = state[0], state[1]
    two = ordered(amps.astype(jnp.bfloat16), other, l // 4)
    other = swap(two, "l", 8, 2)
    quad = gather(block, "h", 4).reshape(4, n, n)
    two, other, quad = lax.optimization_barrier((two, other, quad))
    four = jnp.swapaxes(ordered(two, other, l // 2 % 2), 0, 1).reshape(4, n, n)
    other = swap(four, "l", 8, 1)
    by_y = gather(quad, "y", 4).reshape(16, n, n)
    four, other, by_y = lax.optimization_barrier((four, other, by_y))
    eight = ordered(four, other, l % 2)
    by_l = jnp.swapaxes(eight, 0, 1).reshape(-1, n)
    other = swap(by_y, "c", 2, 1)
    both = ordered(by_y, other, lax.axis_index("c"))
    part = jnp.swapaxes(both, 0, 1).reshape(4, -1, n)

    gap_rows = lax.dynamic_slice_in_dim(orbital_gaps, lax.axis_index(("x", "l")) * n, n)
    shift = sum(jnp.where(h == i, SHIFT[i], 0) for i in range(SIZES[3]))
    col = (lax.axis_index("y") - shift + 4) % 4 * 8 + lax.axis_index(("h", "c"))
    gap_cols = lax.dynamic_slice_in_dim(orbital_gaps, col * n, n)
    delta = gap_rows[:, None] + gap_cols[None, :]
    lane = lax.broadcasted_iota(jnp.int32, (1, 128), 1)
    local = jnp.zeros((1, 128), jnp.float32)
    for step in range(ITERS):
        if step:
            by_l = gather(amps.astype(jnp.bfloat16), "l", 8).reshape(-1, n)
        shares = jnp.einsum("ykr,kc->yrc", part, by_l, preferred_element_type=jnp.float32)
        product = jnp.sum(lax.all_to_all(shares, "x", 0, 0, tiled=True), axis=0)
        mirror = send(product, turned, turned.T)
        if step:
            local = jnp.where(lane == step - 1, square, local)
            mirror, local = lax.optimization_barrier((mirror, local))
        paired = product + mirror.T
        residual = source + delta * amps + paired + amps * paired
        square = jnp.sum(residual * residual)
        amps = amps - residual / delta

    local = jnp.where(lane == ITERS - 1, square, local)
    plane = jnp.sum(gather(local, ("y", "x", "c"), 32), axis=0)
    total = jnp.sum(gather(plane, ("l", "h"), 32), axis=0)
    norms = jnp.sqrt(total[0, :ITERS]) / (NO * NV)
    return (send(amps, turned, start), norms)


def solution(mesh):
    fine = Mesh(mesh.devices.reshape(SIZES), AXES)
    in_specs = (P(ROW, COL), P(ROW, COL), P(ROW, COL), P())
    out_specs = (P(ROW, COL), P())
    return jax.shard_map(body, mesh=fine, in_specs=in_specs, out_specs=out_specs, check_vma=False)
```

```python
import jax
import jax.numpy as jnp
import numpy as np
from jax import lax
from jax.sharding import Mesh, PartitionSpec as P

NO = 16
NV = 256
ITERS = 3

AXES = ("y", "l", "x", "h", "c")
SIZES = (4, 8, 4, 4, 2)
SIDE = 32
ROW = ("y", "l")
COL = ("x", "h", "c")
SHIFT = (0, 0, 0, 2)


def gather(tile, axes, count):
    copies = jnp.broadcast_to(tile[None], (count,) + tile.shape)
    return lax.all_to_all(copies, axes, 0, 0, tiled=True)


def swap(tile, axis, size, bit):
    return lax.ppermute(tile, axis, [(i, i ^ bit) for i in range(size)])


def ordered(own, other, bit):
    first = bit == 0
    return jnp.stack([jnp.where(first, own, other), jnp.where(first, other, own)])


def places():
    grid = np.arange(SIDE * SIDE).reshape(SIZES)
    later = np.zeros(SIZES, np.int64)
    for y, l, x, h, c in np.ndindex(SIZES):
        later[y, l, x, h, c] = grid[(x + SHIFT[h]) % SIZES[0], l, y, h, c]
    return grid.reshape(SIDE, SIDE), later.reshape(SIDE, SIDE)


def send(tile, source, target):
    return lax.ppermute(tile, AXES, list(zip(source.ravel().tolist(), target.ravel().tolist())))


def body(amplitudes, coupling, source, orbital_gaps):
    n = amplitudes.shape[0]
    h = lax.axis_index("h")
    start, turned = places()

    block = coupling.T
    l = lax.axis_index("l")
    low = amplitudes.astype(jnp.bfloat16)
    across = turned[np.arange(SIDE) ^ 4]
    own, other = send(low, start, turned), send(low, start, across)
    two = ordered(own, other, l // 4)
    other = swap(two, "l", 8, 2)
    quad = gather(block, "h", 4).reshape(4, n, n)
    two, other, quad = lax.optimization_barrier((two, other, quad))
    four = jnp.swapaxes(ordered(two, other, l // 2 % 2), 0, 1).reshape(4, n, n)
    other = swap(four, "l", 8, 1)
    by_y = gather(quad, "y", 4).reshape(16, n, n)
    state = send(jnp.stack([source, amplitudes]), start, turned)
    four, other, by_y, state = lax.optimization_barrier((four, other, by_y, state))
    eight = ordered(four, other, l % 2)
    by_l = jnp.swapaxes(eight, 0, 1).reshape(-1, n)
    other = swap(by_y, "c", 2, 1)
    both = ordered(by_y, other, lax.axis_index("c"))
    part = jnp.swapaxes(both, 0, 1).reshape(4, -1, n)

    source, amps = state[0], state[1]
    gap_rows = lax.dynamic_slice_in_dim(orbital_gaps, lax.axis_index(("x", "l")) * n, n)
    shift = sum(jnp.where(h == i, SHIFT[i], 0) for i in range(SIZES[3]))
    col = (lax.axis_index("y") - shift + 4) % 4 * 8 + lax.axis_index(("h", "c"))
    gap_cols = lax.dynamic_slice_in_dim(orbital_gaps, col * n, n)
    delta = gap_rows[:, None] + gap_cols[None, :]
    lane = lax.broadcasted_iota(jnp.int32, (1, 128), 1)
    local = jnp.zeros((1, 128), jnp.float32)
    for step in range(ITERS):
        if step:
            by_l = gather(amps.astype(jnp.bfloat16), "l", 8).reshape(-1, n)
        shares = jnp.einsum("ykr,kc->yrc", part, by_l, preferred_element_type=jnp.float32)
        product = jnp.sum(lax.all_to_all(shares, "x", 0, 0, tiled=True), axis=0)
        mirror = send(product, turned, turned.T)
        if step:
            local = jnp.where(lane == step - 1, square, local)
            mirror, local = lax.optimization_barrier((mirror, local))
        paired = product + mirror.T
        residual = source + delta * amps + paired + amps * paired
        square = jnp.sum(residual * residual)
        amps = amps - residual / delta

    local = jnp.where(lane == ITERS - 1, square, local)
    plane = jnp.sum(gather(local, ("y", "x", "c"), 32), axis=0)
    total = jnp.sum(gather(plane, ("l", "h"), 32), axis=0)
    norms = jnp.sqrt(total[0, :ITERS]) / (NO * NV)
    return (send(amps, turned, start), norms)


def solution(mesh):
    fine = Mesh(mesh.devices.reshape(SIZES), AXES)
    in_specs = (P(ROW, COL), P(ROW, COL), P(ROW, COL), P())
    out_specs = (P(ROW, COL), P())
    return jax.shard_map(body, mesh=fine, in_specs=in_specs, out_specs=out_specs, check_vma=False)
```

```python
import jax
import jax.numpy as jnp
import numpy as np
from jax import lax
from jax.sharding import Mesh, PartitionSpec as P

NO = 16
NV = 256
ITERS = 3

AXES = ("y", "l", "x", "h", "c")
SIZES = (4, 8, 4, 4, 2)
SIDE = 32
ROW = ("y", "l")
COL = ("x", "h", "c")
SHIFT = (0, 0, 0, 2)


def gather(tile, axes, count):
    copies = jnp.broadcast_to(tile[None], (count,) + tile.shape)
    return lax.all_to_all(copies, axes, 0, 0, tiled=True)


def swap(tile, axis, size, bit):
    return lax.ppermute(tile, axis, [(i, i ^ bit) for i in range(size)])


def ordered(own, other, bit):
    first = bit == 0
    return jnp.stack([jnp.where(first, own, other), jnp.where(first, other, own)])


def places():
    grid = np.arange(SIDE * SIDE).reshape(SIZES)
    later = np.zeros(SIZES, np.int64)
    for y, l, x, h, c in np.ndindex(SIZES):
        later[y, l, x, h, c] = grid[(x + SHIFT[h]) % SIZES[0], l, y, h, c]
    return grid.reshape(SIDE, SIDE), later.reshape(SIDE, SIDE)


def send(tile, source, target):
    return lax.ppermute(tile, AXES, list(zip(source.ravel().tolist(), target.ravel().tolist())))


def body(amplitudes, coupling, source, orbital_gaps):
    n = amplitudes.shape[0]
    h = lax.axis_index("h")
    start, turned = places()

    block = coupling.T
    l = lax.axis_index("l")
    low = amplitudes.astype(jnp.bfloat16)
    across = turned[np.arange(SIDE) ^ 4]
    own, other = send(low, start, turned), send(low, start, across)
    two = ordered(own, other, l // 4)
    other = swap(two, "l", 8, 2)
    quad = gather(block, "h", 4).reshape(4, n, n)
    two, other, quad = lax.optimization_barrier((two, other, quad))
    four = jnp.swapaxes(ordered(two, other, l // 2 % 2), 0, 1).reshape(4, n, n)
    other = swap(four, "l", 8, 1)
    by_y = gather(quad, "y", 4).reshape(16, n, n)
    state = send(jnp.stack([source, amplitudes]), start, turned)
    four, other, by_y, state = lax.optimization_barrier((four, other, by_y, state))
    eight = ordered(four, other, l % 2)
    by_l = jnp.swapaxes(eight, 0, 1).reshape(-1, n)
    other = swap(by_y, "c", 2, 1)
    both = ordered(by_y, other, lax.axis_index("c"))
    part = jnp.swapaxes(both, 0, 1).reshape(4, -1, n)

    source, amps = state[0], state[1]
    gap_rows = lax.dynamic_slice_in_dim(orbital_gaps, lax.axis_index(("x", "l")) * n, n)
    shift = sum(jnp.where(h == i, SHIFT[i], 0) for i in range(SIZES[3]))
    col = (lax.axis_index("y") - shift + 4) % 4 * 8 + lax.axis_index(("h", "c"))
    gap_cols = lax.dynamic_slice_in_dim(orbital_gaps, col * n, n)
    delta = gap_rows[:, None] + gap_cols[None, :]
    lane = lax.broadcasted_iota(jnp.int32, (1, 128), 1)
    local = jnp.zeros((1, 128), jnp.float32)
    for step in range(ITERS):
        if step:
            by_l = gather(amps.astype(jnp.bfloat16), "l", 8).reshape(-1, n)
        shares = jnp.einsum("ykr,kc->yrc", part, by_l, preferred_element_type=jnp.float32)
        product = jnp.sum(lax.all_to_all(shares, "x", 0, 0, tiled=True), axis=0)
        mirror = send(product, turned, turned.T)
        if step:
            local = jnp.where(lane == step - 1, square, local)
            mirror, local = lax.optimization_barrier((mirror, local))
        paired = product + mirror.T
        residual = source + delta * amps + paired + amps * paired
        square = jnp.sum(residual * residual)
        amps = amps - residual / delta

    local = jnp.where(lane == ITERS - 1, square, local)
    moved = send(amps, turned, start)
    plane, moved = lax.optimization_barrier((gather(local, ("y", "x", "c"), 32), moved))
    plane = jnp.sum(plane, axis=0)
    total = jnp.sum(gather(plane, ("l", "h"), 32), axis=0)
    norms = jnp.sqrt(total[0, :ITERS]) / (NO * NV)
    return (moved, norms)


def solution(mesh):
    fine = Mesh(mesh.devices.reshape(SIZES), AXES)
    in_specs = (P(ROW, COL), P(ROW, COL), P(ROW, COL), P())
    out_specs = (P(ROW, COL), P())
    return jax.shard_map(body, mesh=fine, in_specs=in_specs, out_specs=out_specs, check_vma=False)
```
